512 devices in a mesh: dp: 16 (over z_hi, x), st: 32 (over y, z_lo, core).
Axes of the slice: x: 4, y: 8, z: 8 (z_hi: 4, z_lo: 2; z = z_hi * 2 + z_lo), core: 2. Of those that a mesh axis runs over, the one named last changes fastest.
Arguments:
- grad_out: bfloat16 [4096, 8192], P(('dp', 'st')), may hold values from -6 to 6
- w_down: bfloat16 [26624, 8192], P('st', 'dp'), may hold values from -0.0625 to 0.0625
- gate_pre: bfloat16 [4096, 26624], P('dp', 'st'), may hold values from -8 to 8
- up_pre: bfloat16 [4096, 26624], P('dp', 'st'), may hold values from -6 to 6
- rank_in: bfloat16 [4096, 128], P(('dp', 'st')), may hold values from -0.09375 to 0.09375
- rank_hidden: bfloat16 [4096, 64], P(('dp', 'st')), may hold values from -0.09375 to 0.09375
- a_down: bfloat16 [26624, 64], P('st'), may hold values from -0.75 to 0.75
- b_down: bfloat16 [64, 8192], P(None, 'st'), may hold values from -0.0625 to 0.0625
- b_in: bfloat16 [2, 64, 26624], P(None, None, 'st'), may hold values from -0.0390625 to 0.0390625
- a_in: bfloat16 [8192, 128], replicated, may hold values from -0.75 to 0.75
Outputs:
- input_grad: bfloat16 [4096, 8192], P(('dp', 'st'))
- grad_b_in: float32 [2, 64, 26624], P(None, None, 'st')
- grad_b_down: float32 [64, 8192], P(None, 'st')
The draws below stay inside these ranges and needn't reach their ends.
All inputs are finite; a program needn't handle non-finite values.
Results may differ from the reference program's by a relative error of at most 0.009.
Values may be sent and summed in bfloat16 or wider, within the bound.
No kernel may reach another device: no remote copies, remote signals or barrier semaphores. Data moves between devices by JAX's collectives and lax.ppermute only.
A program may use at most 64 MiB of HBM per device.

```python
import jax
import jax.numpy as jnp

D = 8192
FF = 26624
R = 64
TOKENS = 4096


def block_levels(key, dims, split, least, top_value):
    level, own = 1.0, jax.random.fold_in(key, 6)
    for position, shards_of in split:
        draws = jnp.exp(jax.random.uniform(jax.random.fold_in(own, position), (shards_of,), jnp.float32, least / len(split), top_value / len(split)))
        level = level * jnp.repeat(draws, dims[position] // shards_of).reshape([-1 if axis == position else 1 for axis in range(len(dims))])
    return level


def scatter_about(rng, extent, scale, most, cuts=(), dtype=jnp.bfloat16):
    array = jax.random.normal(rng, extent, jnp.float32) * scale
    if len(cuts) > 0:
        array = block_levels(rng, extent, cuts, -0.22, 0.18) * array
    return jnp.clip(array, min=-most, max=most).astype(dtype)


def setup_inputs(seed: int = 0) -> dict:
    keys = jax.random.split(jax.random.key(seed), 11)
    return {
        "grad_out": scatter_about(keys[0], (TOKENS, D), 1.0, 6.0, ((0, 512),)),
        "w_down": scatter_about(keys[1], (FF, D), D ** -0.5, 0.0625, ((0, 32), (1, 16))),
        "gate_pre": scatter_about(keys[2], (TOKENS, FF), 2.0, 8.0, ((0, 16), (1, 32))),
        "up_pre": scatter_about(keys[3], (TOKENS, FF), 1.0, 6.0, ((0, 16), (1, 32))),
        "rank_in": scatter_about(keys[4], (TOKENS, 2 * R), TOKENS ** -0.5, 0.09375, ((0, 512),)),
        "rank_hidden": scatter_about(keys[5], (TOKENS, R), TOKENS ** -0.5, 0.09375, ((0, 512),)),
        "a_down": scatter_about(keys[6], (FF, R), R ** -0.5, 0.75, ((0, 32),)),
        "b_down": scatter_about(keys[7], (R, D), D ** -0.5, 0.0625, ((1, 32),)),
        "b_in": scatter_about(keys[8], (2, R, FF), FF ** -0.5, 0.0390625, ((2, 32),)),
        "a_in": scatter_about(keys[9], (D, 2 * R), R ** -0.5, 0.75),
    }


def reference(grad_out, w_down, gate_pre, up_pre, rank_in, rank_hidden, a_down, b_down, b_in, a_in):
    frozen = jnp.dot(grad_out, w_down.T, preferred_element_type=jnp.float32)
    down_rank = jnp.dot(grad_out, b_down.T, preferred_element_type=jnp.float32).astype(jnp.bfloat16)
    grad_hidden = frozen + jnp.dot(down_rank, a_down.T, preferred_element_type=jnp.float32)
    gate_value = gate_pre.astype(jnp.float32)
    up_value = up_pre.astype(jnp.float32)
    sigmoid_gate = jax.nn.sigmoid(gate_value)
    grad_up = (grad_hidden * gate_value * sigmoid_gate).astype(jnp.bfloat16)
    grad_gate = (grad_hidden * up_value * sigmoid_gate * (1.0 + gate_value * (1.0 - sigmoid_gate))).astype(jnp.bfloat16)
    grad_b_gate = jnp.dot(rank_in[:, :R].T, grad_gate, preferred_element_type=jnp.float32)
    grad_b_up = jnp.dot(rank_in[:, R:].T, grad_up, preferred_element_type=jnp.float32)
    grad_b_in = jnp.stack([grad_b_gate, grad_b_up])
    grad_b_down = jnp.dot(rank_hidden.T, grad_out, preferred_element_type=jnp.float32)
    rank_gate = jnp.dot(grad_gate, b_in[0].T, preferred_element_type=jnp.float32)
    rank_up = jnp.dot(grad_up, b_in[1].T, preferred_element_type=jnp.float32)
    rank_grad = jnp.concatenate([rank_gate, rank_up], axis=1).astype(jnp.bfloat16)
    input_grad = jnp.dot(rank_grad, a_in.T, preferred_element_type=jnp.float32).astype(jnp.bfloat16)
    return input_grad, grad_b_in, grad_b_down
```

```python
import jax
import jax.numpy as jnp
import numpy as np
from jax import lax
from jax.sharding import Mesh, PartitionSpec as P

AXES = ("zh", "x", "yh", "yl", "zl", "c")
SIZES = (4, 4, 4, 2, 2, 2)
Y = ("yh", "yl")
DP = ("zh", "x")
ST = ("yh", "yl", "zl", "c")
TOKEN_ORDER = ("c", "yh", "yl", "zl")
F32, BF16 = jnp.float32, jnp.bfloat16


def contract_last(left, right):
    return lax.dot_general(left, right, (((1,), (1,)), ((), ())), preferred_element_type=F32)


def contract_first(left, right):
    return lax.dot_general(left, right, (((0,), (0,)), ((), ())), preferred_element_type=F32)


def exchange(blocks, axes):
    return lax.all_to_all(blocks, axes, 0, 0, tiled=True)


def spread(block, axes, count):
    return exchange(jnp.broadcast_to(block[None], (count,) + block.shape), axes)


def band_pairs():
    index = np.arange(512).reshape(SIZES)
    pairs = []
    for zh in range(4):
        for x in range(4):
            for yh in range(4):
                for yl in range(2):
                    for zl in range(2):
                        for c in range(2):
                            pairs.append((int(index[yh, x, zh, yl, zl, c]), int(index[zh, x, yh, yl, zl, c])))
    return pairs


def shards(grad_out, w_down, gate_pre, up_pre, rank_in, rank_hidden, a_down, b_down, b_in, a_in):
    quarters = grad_out.reshape(8, 4, 2048).transpose(1, 0, 2)
    to_z = jnp.broadcast_to(quarters[:, None], (4, 2, 8, 2048)).reshape(8, 8, 2048)
    from_z = exchange(to_z, ("zh", "zl")).reshape(4, 16, 2048)
    from_y = lax.all_gather(from_z, Y, axis=1, tiled=True)
    grad_rows = lax.all_gather(from_y, "c", axis=1, tiled=True)
    w_blocks = spread(w_down, "x", 4)
    own_band = lax.ppermute(b_down, AXES, band_pairs())
    bands = spread(own_band, ("yl", "zl", "c"), 8).transpose(1, 0, 2).reshape(64, 2048)
    weights = w_blocks.transpose(1, 0, 2).reshape(832, 2048).astype(F32)
    weights = (weights + jnp.dot(a_down, bands, preferred_element_type=F32)).astype(BF16)
    ranks = jnp.concatenate([rank_in, rank_hidden], axis=1)
    ranks = spread(spread(ranks, "zh", 4), TOKEN_ORDER, 32)
    ranks = ranks.transpose(1, 0, 2, 3).reshape(4, 256, 192)
    saved_in = lax.dynamic_index_in_dim(ranks, lax.axis_index("zh"), 0, False)[:, :128]
    saved_hidden = ranks[:, :, 128:].reshape(1024, 64)
    rows = grad_rows.reshape(1024, 2048)
    partial = contract_last(rows, weights).astype(BF16).reshape(4, 256, 832)
    grad_hidden = jnp.sum(exchange(partial, "zh").astype(F32), axis=0)

    def by_token(saved):
        return saved.reshape(16, 2, 8, 832).transpose(1, 0, 2, 3).reshape(256, 832).astype(F32)

    gate_value, up_value = by_token(gate_pre), by_token(up_pre)
    sigmoid_gate = jax.nn.sigmoid(gate_value)
    grad_up = (grad_hidden * gate_value * sigmoid_gate).astype(BF16)
    grad_gate = (
        grad_hidden * up_value * sigmoid_gate * (1.0 + gate_value * (1.0 - sigmoid_gate))
    ).astype(BF16)
    partial_in = jnp.concatenate(
        [contract_first(saved_in[:, :64], grad_gate), contract_first(saved_in[:, 64:], grad_up)], axis=0
    )
    station = lax.axis_index(ST)
    band = lax.dynamic_slice_in_dim(rows, (station % 8) * 256, 256, 1)
    partial_down = contract_first(saved_hidden, band)
    partial_down = jnp.where(station // 8 == lax.axis_index("zh"), partial_down, 0.0)
    sums = jnp.concatenate([partial_in.reshape(16, 8, 832), partial_down.reshape(16, 8, 128)], axis=2)
    sums = jnp.sum(exchange(sums.astype(BF16), DP).astype(F32), axis=0).astype(BF16)
    sums = spread(sums, DP, 16).astype(F32)
    grad_b_in = sums[:, :, :832].reshape(2, 64, 832)
    grad_b_down = sums[:, :, 832:].reshape(64, 256)
    rank_partial = jnp.concatenate(
        [contract_last(grad_gate, b_in[0]), contract_last(grad_up, b_in[1])], axis=1
    )
    rank_grad = jnp.sum(exchange(rank_partial.reshape(32, 8, 128), TOKEN_ORDER), axis=0).astype(BF16)
    input_grad = contract_last(rank_grad, a_in).astype(BF16)
    return (input_grad, grad_b_in, grad_b_down)


def solution(mesh):
    fine = Mesh(mesh.devices.reshape(SIZES), AXES)
    placed = (
        P(AXES, None),
        P(ST, DP),
        P(DP, ST),
        P(DP, ST),
        P(AXES, None),
        P(AXES, None),
        P(ST, None),
        P(None, ST),
        P(None, None, ST),
        P(),
    )
    return jax.shard_map(
        shards,
        mesh=fine,
        in_specs=placed,
        out_specs=(P(AXES, None), P(None, None, ST), P(None, ST)),
        check_vma=False,
    )
```

```python
import jax
import jax.numpy as jnp
import numpy as np
from jax import lax
from jax.experimental import pallas as pl
from jax.experimental.pallas import tpu as pltpu
from jax.sharding import Mesh, PartitionSpec as P

AXES = ("zh", "x", "yh", "yl", "zl", "c")
SIZES = (4, 4, 4, 2, 2, 2)
Y = ("yh", "yl")
DP = ("zh", "x")
ST = ("yh", "yl", "zl", "c")
TOKEN_ORDER = ("c", "yh", "yl", "zl")
F32, BF16 = jnp.float32, jnp.bfloat16
VMEM = pl.BlockSpec(memory_space=pltpu.VMEM)
PARAMS = pltpu.CompilerParams(vmem_limit_bytes=56 * 2**20)


def contract_last(left, right):
    return lax.dot_general(left, right, (((1,), (1,)), ((), ())), preferred_element_type=F32)


def contract_first(left, right):
    return lax.dot_general(left, right, (((0,), (0,)), ((), ())), preferred_element_type=F32)


def exchange(blocks, axes):
    return lax.all_to_all(blocks, axes, 0, 0, tiled=True)


def spread(block, axes, count):
    return exchange(jnp.broadcast_to(block[None], (count,) + block.shape), axes)


def swap_cores(array):
    return lax.ppermute(array, "c", [(0, 1), (1, 0)])


def band_pairs():
    index = np.arange(512).reshape(SIZES)
    pairs = []
    for zh in range(4):
        for x in range(4):
            for yh in range(4):
                for yl in range(2):
                    for zl in range(2):
                        for c in range(2):
                            source = index[yh, yl * 2 + zl, zh, x // 2, x % 2, c]
                            pairs.append((int(source), int(index[zh, x, yh, yl, zl, c])))
    return pairs


def partial_hidden(rows, weights, a_down):
    rows = rows[:, :2048].reshape(512, 4, 512)
    total = lax.dot_general(weights, rows, (((0, 2), (1, 2)), ((), ())), preferred_element_type=F32)
    rank = total[832:].astype(BF16)
    whole = total[:832] + jnp.dot(a_down, rank, preferred_element_type=F32)
    return whole.astype(BF16).reshape(832, 4, 128).transpose(1, 0, 2)


def adapter_terms(parts_ref, gate_ref, up_ref, saved_ref, b_gate_ref, b_up_ref):
    grad_hidden = jnp.sum(parts_ref[...].astype(F32), axis=0)
    grad_gate = (grad_hidden * gate_ref[...]).astype(BF16)
    grad_up = (grad_hidden * up_ref[...]).astype(BF16)
    rank = jnp.dot(b_gate_ref[...], grad_gate, preferred_element_type=F32)
    rank = rank + jnp.dot(b_up_ref[...], grad_up, preferred_element_type=F32)
    into_gate = contract_last(saved_ref[:64, :], grad_gate)
    into_up = contract_last(saved_ref[64:, :], grad_up)
    return rank.T, into_gate, into_up


def own_kernel(parts_ref, gate_ref, up_ref, saved_ref, b_gate_ref, b_up_ref, rank_ref, sums_ref):
    rank, into_gate, into_up = adapter_terms(parts_ref, gate_ref, up_ref, saved_ref, b_gate_ref, b_up_ref)
    rank_ref[...] = rank
    sums_ref[:64, :] = into_gate
    sums_ref[64:, :] = into_up


def other_kernel(
    core_ref, parts_ref, gate_ref, up_ref, saved_ref, b_gate_ref, b_up_ref, own_rank_ref, own_sums_ref, down_ref, rank_ref, sums_ref
):
    rank, into_gate, into_up = adapter_terms(parts_ref, gate_ref, up_ref, saved_ref, b_gate_ref, b_up_ref)
    core = core_ref[0]
    rank_ref[core] = own_rank_ref[...]
    rank_ref[1 - core] = rank
    sums_ref[:, :128] = down_ref[...]
    sums_ref[:64, 128:] = (own_sums_ref[:64, :] + into_gate).astype(BF16)
    sums_ref[64:, 128:] = (own_sums_ref[64:, :] + into_up).astype(BF16)


def own_terms(*operands):
    return pl.pallas_call(
        own_kernel,
        out_shape=(jax.ShapeDtypeStruct((128, 128), F32), jax.ShapeDtypeStruct((128, 832), F32)),
        in_specs=[VMEM] * 6,
        out_specs=(VMEM, VMEM),
        compiler_params=PARAMS,
        cost_estimate=pl.CostEstimate(flops=10**8, bytes_accessed=3 * 2**20, transcendentals=0),
    )(*operands)


def other_terms(*operands):
    return pl.pallas_call(
        other_kernel,
        out_shape=(jax.ShapeDtypeStruct((2, 128, 128), F32), jax.ShapeDtypeStruct((128, 960), BF16)),
        in_specs=[pl.BlockSpec(memory_space=pltpu.SMEM)] + [VMEM] * 9,
        out_specs=(VMEM, VMEM),
        compiler_params=PARAMS,
        cost_estimate=pl.CostEstimate(flops=10**8, bytes_accessed=3 * 2**20, transcendentals=0),
    )(*operands)


def factor_kernel(core_ref, gate_ref, up_ref, gate_out, up_out):
    core = core_ref[0]
    gate_rows = gate_ref[...].astype(F32).reshape(16, 2, 8, 832)
    up_rows = up_ref[...].astype(F32).reshape(16, 2, 8, 832)
    for which in range(2):
        slot = core if which == 0 else 1 - core
        gate_value = gate_rows[:, which].reshape(128, 832)
        sigmoid_gate = jax.nn.sigmoid(gate_value)
        up_out[slot] = (gate_value * sigmoid_gate).T
        slope = sigmoid_gate * (1.0 + gate_value * (1.0 - sigmoid_gate))
        gate_out[slot] = (up_rows[:, which].reshape(128, 832) * slope).T


def factors(core, gate_pre, up_pre):
    shape = jax.ShapeDtypeStruct((2, 832, 128), F32)
    return pl.pallas_call(
        factor_kernel,
        out_shape=(shape, shape),
        in_specs=[pl.BlockSpec(memory_space=pltpu.SMEM), VMEM, VMEM],
        out_specs=(VMEM, VMEM),
        compiler_params=PARAMS,
        cost_estimate=pl.CostEstimate(flops=10**7, bytes_accessed=3 * 2**20, transcendentals=256 * 832),
    )(core.reshape(1), gate_pre, up_pre)


def saved_kernel(place_ref, own_band_ref, other_band_ref, own_ranks_ref, other_ranks_ref, saved_ref, down_ref):
    down = contract_first(own_ranks_ref[:, 128:192], own_band_ref[...])
    down = down + contract_first(other_ranks_ref[:, 128:192], other_band_ref[...])
    down_ref[...] = jnp.where(place_ref[2] == 1, down, 0.0).astype(BF16)
    window = pl.ds(pl.multiple_of(place_ref[1] * 128, 128), 128)
    saved_ref[0] = own_ranks_ref[window, :128].T
    saved_ref[1] = other_ranks_ref[window, :128].T


def saved_terms(place, own_rows, other_rows):
    band = pl.BlockSpec((512, 256), lambda i, place: (0, place[0]))
    ranks = pl.BlockSpec((512, 256), lambda i, place: (0, 8))
    return pl.pallas_call(
        saved_kernel,
        grid_spec=pltpu.PrefetchScalarGridSpec(
            num_scalar_prefetch=1,
            grid=(1,),
            in_specs=[band, band, ranks, ranks],
            out_specs=(
                pl.BlockSpec((2, 128, 128), lambda i, place: (0, 0, 0)),
                pl.BlockSpec((64, 256), lambda i, place: (0, 0)),
            ),
        ),
        out_shape=(jax.ShapeDtypeStruct((2, 128, 128), BF16), jax.ShapeDtypeStruct((64, 256), BF16)),
        compiler_params=PARAMS,
        cost_estimate=pl.CostEstimate(flops=2 * 1024 * 64 * 256, bytes_accessed=2**20, transcendentals=0),
    )(place, own_rows, other_rows, own_rows, other_rows)


def shards(grad_out, w_down, gate_pre, up_pre, rank_in, rank_hidden, a_down, b_down, b_in, a_in):
    core = lax.axis_index("c")
    zh = lax.axis_index("zh")
    station = lax.axis_index(ST)

    ranks = jnp.concatenate([rank_in, rank_hidden, jnp.zeros((8, 64), BF16)], axis=1)
    quarters = grad_out.reshape(8, 4, 2048).transpose(1, 0, 2)
    quarters = jnp.concatenate([quarters, jnp.broadcast_to(ranks[None], (4, 8, 256))], axis=2)
    blocks = jnp.broadcast_to(quarters[:, None], (4, 2, 8, 2304)).reshape(8, 8, 2304)
    own_band = lax.ppermute(b_down, AXES, band_pairs())
    other_band = swap_cores(own_band)
    band_pair = jnp.where(
        core == 0, jnp.concatenate([own_band, other_band], axis=1), jnp.concatenate([other_band, own_band], axis=1)
    )
    w_here = jnp.concatenate([w_down, band_pair])
    from_z = exchange(blocks, ("zh", "zl"))
    gate_factor, up_factor = factors(core, gate_pre, up_pre)
    none = jnp.zeros((64, 832), BF16)
    b_gate, b_up = jnp.concatenate([b_in[0], none]), jnp.concatenate([none, b_in[1]])
    ready = (from_z, w_here, gate_factor, up_factor, b_gate, b_up, a_down)
    from_z, w_here, gate_factor, up_factor, b_gate, b_up, a_down = lax.optimization_barrier(ready)
    own_rows = lax.all_gather(from_z.reshape(4, 16, 2304), Y, axis=1, tiled=True).reshape(512, 2304)
    weights = spread(w_here, "x", 4)
    own_rows, weights = lax.optimization_barrier((own_rows, weights))
    other_rows = swap_cores(own_rows)

    own_parts = exchange(partial_hidden(own_rows, weights, a_down), "zh")
    other_partial = partial_hidden(other_rows, weights, a_down)
    other_parts = exchange(other_partial, "zh")

    place = jnp.stack([station % 8, zh, (station // 8 == zh).astype(jnp.int32)])
    place, _ = lax.optimization_barrier((place, other_partial))
    saved, partial_down = saved_terms(place, own_rows, other_rows)
    partial_down = partial_down.reshape(128, 128)
    own_rank, own_sums = own_terms(own_parts, gate_factor[0], up_factor[0], saved[0], b_gate, b_up)
    rank_partial, sums = other_terms(
        core.reshape(1), other_parts, gate_factor[1], up_factor[1], saved[1], b_gate, b_up, own_rank, own_sums, partial_down
    )
    sums = jnp.sum(exchange(sums.reshape(16, 8, 960), DP).astype(F32), axis=0).astype(BF16)
    rank_partial, sums = lax.optimization_barrier((rank_partial, sums))
    rank_grad = jnp.sum(exchange(rank_partial.reshape(32, 8, 128), TOKEN_ORDER), axis=0).astype(BF16)
    sums = spread(sums, DP, 16).astype(F32)
    grad_b_in = sums[:, :, 128:].reshape(2, 64, 832)
    grad_b_down = sums[:, :, :128].reshape(64, 256)
    input_grad = contract_last(rank_grad, a_in).astype(BF16)
    return (input_grad, grad_b_in, grad_b_down)


def solution(mesh):
    fine = Mesh(mesh.devices.reshape(SIZES), AXES)
    placed = (
        P(AXES, None),
        P(ST, DP),
        P(DP, ST),
        P(DP, ST),
        P(AXES, None),
        P(AXES, None),
        P(ST, None),
        P(None, ST),
        P(None, None, ST),
        P(),
    )
    return jax.shard_map(
        shards,
        mesh=fine,
        in_specs=placed,
        out_specs=(P(AXES, None), P(None, None, ST), P(None, ST)),
        check_vma=False,
    )
```

```python
import jax
import jax.numpy as jnp
import numpy as np
from jax import lax
from jax.experimental import pallas as pl
from jax.experimental.pallas import tpu as pltpu
from jax.sharding import Mesh, PartitionSpec as P

AXES = ("zh", "x", "yh", "yl", "zl", "c")
SIZES = (4, 4, 4, 2, 2, 2)
Y = ("yh", "yl")
DP = ("zh", "x")
ST = ("yh", "yl", "zl", "c")
F32, BF16 = jnp.float32, jnp.bfloat16
VMEM = pl.BlockSpec(memory_space=pltpu.VMEM)
PARAMS = pltpu.CompilerParams(vmem_limit_bytes=56 * 2**20)


def contract_last(left, right):
    return lax.dot_general(left, right, (((1,), (1,)), ((), ())), preferred_element_type=F32)


def contract_first(left, right):
    return lax.dot_general(left, right, (((0,), (0,)), ((), ())), preferred_element_type=F32)


def exchange(blocks, axes):
    return lax.all_to_all(blocks, axes, 0, 0, tiled=True)


def spread(block, axes, count):
    return exchange(jnp.broadcast_to(block[None], (count,) + block.shape), axes)


def swap_cores(array):
    return lax.ppermute(array, "c", [(0, 1), (1, 0)])


def halve(array, dim, axis, size, bit):
    mine = lax.axis_index(axis) // bit % 2
    kept = lax.dynamic_index_in_dim(array, mine, dim, False)
    sent = lax.dynamic_index_in_dim(array, 1 - mine, dim, False)
    return kept + lax.ppermute(sent, axis, [(i, i ^ bit) for i in range(size)])


def band_pairs():
    index = np.arange(512).reshape(SIZES)
    pairs = []
    for zh in range(4):
        for x in range(4):
            for yh in range(4):
                for yl in range(2):
                    for zl in range(2):
                        for c in range(2):
                            source = index[x, zl * 2 + c, zh, yh // 2, yh % 2, yl]
                            pairs.append((int(source), int(index[zh, x, yh, yl, zl, c])))
    return pairs


def partial_hidden(rows, weights, a_down):
    rows = rows[:, :2048].reshape(512, 4, 512)
    total = lax.dot_general(weights, rows, (((0, 2), (1, 2)), ((), ())), preferred_element_type=F32)
    rank = total[832:].astype(BF16)
    whole = total[:832] + jnp.dot(a_down, rank, preferred_element_type=F32)
    return whole.astype(BF16).reshape(832, 4, 128).transpose(1, 0, 2)


def adapter_kernel(
    parts_ref, gate_ref, up_ref, saved_ref, b_gate_ref, b_up_ref, down_ref, own_rank_ref, other_rank_ref, sums_ref
):
    into_gate = jnp.zeros((64, 832), F32)
    into_up = jnp.zeros((64, 832), F32)
    for slot, rank_ref in enumerate((own_rank_ref, other_rank_ref)):
        grad_hidden = jnp.sum(parts_ref[:, slot].astype(F32), axis=0)
        grad_gate = (grad_hidden * gate_ref[slot]).astype(BF16)
        grad_up = (grad_hidden * up_ref[slot]).astype(BF16)
        rank = jnp.dot(b_gate_ref[...], grad_gate, preferred_element_type=F32)
        rank = rank + jnp.dot(b_up_ref[...], grad_up, preferred_element_type=F32)
        rank_ref[...] = rank.T
        into_gate = into_gate + contract_last(saved_ref[slot, :64, :], grad_gate)
        into_up = into_up + contract_last(saved_ref[slot, 64:, :], grad_up)
    sums_ref[:, :128] = down_ref[...]
    sums_ref[:64, 128:] = into_gate.astype(BF16)
    sums_ref[64:, 128:] = into_up.astype(BF16)


def adapter_terms(*operands):
    rank = jax.ShapeDtypeStruct((128, 128), F32)
    return pl.pallas_call(
        adapter_kernel,
        out_shape=(rank, rank, jax.ShapeDtypeStruct((128, 960), BF16)),
        in_specs=[VMEM] * 7,
        out_specs=(VMEM, VMEM, VMEM),
        compiler_params=PARAMS,
        cost_estimate=pl.CostEstimate(flops=2 * 10**8, bytes_accessed=5 * 2**20, transcendentals=0),
    )(*operands)


def factor_kernel(core_ref, gate_ref, up_ref, gate_out, up_out):
    core = core_ref[0]
    gate_rows = gate_ref[...].astype(F32).reshape(16, 2, 8, 832)
    up_rows = up_ref[...].astype(F32).reshape(16, 2, 8, 832)
    for which in range(2):
        slot = core if which == 0 else 1 - core
        gate_value = gate_rows[:, which].reshape(128, 832)
        sigmoid_gate = jax.nn.sigmoid(gate_value)
        up_out[slot] = (gate_value * sigmoid_gate).T
        slope = sigmoid_gate * (1.0 + gate_value * (1.0 - sigmoid_gate))
        gate_out[slot] = (up_rows[:, which].reshape(128, 832) * slope).T


def factors(core, gate_pre, up_pre):
    shape = jax.ShapeDtypeStruct((2, 832, 128), F32)
    return pl.pallas_call(
        factor_kernel,
        out_shape=(shape, shape),
        in_specs=[pl.BlockSpec(memory_space=pltpu.SMEM), VMEM, VMEM],
        out_specs=(VMEM, VMEM),
        compiler_params=PARAMS,
        cost_estimate=pl.CostEstimate(flops=10**7, bytes_accessed=3 * 2**20, transcendentals=256 * 832),
    )(core.reshape(1), gate_pre, up_pre)


def saved_kernel(place_ref, own_band_ref, other_band_ref, own_ranks_ref, other_ranks_ref, saved_ref, down_ref):
    down = contract_first(own_ranks_ref[:, 128:192], own_band_ref[...])
    down = down + contract_first(other_ranks_ref[:, 128:192], other_band_ref[...])
    down_ref[...] = jnp.where(place_ref[2] == 1, down, 0.0).astype(BF16)
    window = pl.ds(pl.multiple_of(place_ref[1] * 128, 128), 128)
    saved_ref[0] = own_ranks_ref[window, :128].T
    saved_ref[1] = other_ranks_ref[window, :128].T


def saved_terms(place, own_rows, other_rows):
    band = pl.BlockSpec((512, 256), lambda i, place: (0, place[0]))
    ranks = pl.BlockSpec((512, 256), lambda i, place: (0, 8))
    return pl.pallas_call(
        saved_kernel,
        grid_spec=pltpu.PrefetchScalarGridSpec(
            num_scalar_prefetch=1,
            grid=(1,),
            in_specs=[band, band, ranks, ranks],
            out_specs=(
                pl.BlockSpec((2, 128, 128), lambda i, place: (0, 0, 0)),
                pl.BlockSpec((64, 256), lambda i, place: (0, 0)),
            ),
        ),
        out_shape=(jax.ShapeDtypeStruct((2, 128, 128), BF16), jax.ShapeDtypeStruct((64, 256), BF16)),
        compiler_params=PARAMS,
        cost_estimate=pl.CostEstimate(flops=2 * 1024 * 64 * 256, bytes_accessed=2**20, transcendentals=0),
    )(place, own_rows, other_rows, own_rows, other_rows)


def shards(grad_out, w_down, gate_pre, up_pre, rank_in, rank_hidden, a_down, b_down, b_in, a_in):
    core = lax.axis_index("c")
    zh = lax.axis_index("zh")
    station = lax.axis_index(ST)

    ranks = jnp.concatenate([rank_in, rank_hidden, jnp.zeros((8, 64), BF16)], axis=1)
    quarters = grad_out.reshape(8, 4, 2048).transpose(1, 0, 2)
    quarters = jnp.concatenate([quarters, jnp.broadcast_to(ranks[None], (4, 8, 256))], axis=2)
    blocks = jnp.broadcast_to(quarters[:, None], (4, 2, 8, 2304)).reshape(8, 8, 2304)
    from_z = exchange(blocks, ("zh", "zl"))
    gate_factor, up_factor = factors(core, gate_pre, up_pre)
    none = jnp.zeros((64, 832), BF16)
    b_gate, b_up = jnp.concatenate([b_in[0], none]), jnp.concatenate([none, b_in[1]])
    b_down, b_gate, b_up = lax.optimization_barrier((b_down, b_gate, b_up))
    own_band = lax.ppermute(b_down, AXES, band_pairs()).reshape(4, 16, 256)
    w_copies = jnp.broadcast_to(w_down[None], (4, 832, 512))
    from_z, w_copies = lax.optimization_barrier((from_z, w_copies))
    own = lax.all_gather(jnp.concatenate([from_z.reshape(4, 16, 2304), own_band], axis=2), Y, axis=1, tiled=True)
    weights = exchange(w_copies.reshape(3328, 512), "x").reshape(4, 832, 512)
    bands = own[:, :, 2304:].reshape(4, 8, 16, 256).transpose(1, 0, 2, 3).reshape(4, 2, 64, 256)
    bands = bands.transpose(0, 2, 1, 3).reshape(4, 64, 512)
    own, gate_factor, up_factor, a_down = lax.optimization_barrier((own, gate_factor, up_factor, a_down))
    own_rows = own.reshape(512, 2560)
    other_rows = swap_cores(own_rows)
    weights = jnp.concatenate([weights, bands], axis=1)
    own_partial = partial_hidden(own_rows, weights, a_down)
    other_partial = partial_hidden(other_rows, weights, a_down)
    parts = exchange(jnp.stack([own_partial, other_partial], axis=1), "zh")

    place = jnp.stack([station % 8, zh, (station // 8 == zh).astype(jnp.int32)])
    place, _ = lax.optimization_barrier((place, other_partial))
    saved, partial_down = saved_terms(place, own_rows, other_rows)
    partial_down = partial_down.reshape(128, 128)
    own_rank, other_rank, sums = adapter_terms(parts, gate_factor, up_factor, saved, b_gate, b_up, partial_down)
    sums = jnp.sum(exchange(sums.reshape(16, 8, 960), DP).astype(F32), axis=0).astype(BF16)
    rank_grad = (own_rank + swap_cores(other_rank)).reshape(8, 2, 8, 128)
    rank_grad = halve(rank_grad, 1, "zl", 2, 1)
    rank_grad = halve(rank_grad.reshape(4, 2, 8, 128), 1, "yl", 2, 1)
    rank_grad = halve(rank_grad.reshape(2, 2, 8, 128), 1, "yh", 4, 1)
    rank_grad = halve(rank_grad.reshape(2, 8, 128), 0, "yh", 4, 2)
    rank_grad = rank_grad.astype(BF16)
    sums = spread(sums, DP, 16).astype(F32)
    grad_b_in = sums[:, :, 128:].reshape(2, 64, 832)
    grad_b_down = sums[:, :, :128].reshape(64, 256)
    input_grad = contract_last(rank_grad, a_in).astype(BF16)
    return (input_grad, grad_b_in, grad_b_down)


def solution(mesh):
    fine = Mesh(mesh.devices.reshape(SIZES), AXES)
    placed = (
        P(AXES, None),
        P(ST, DP),
        P(DP, ST),
        P(DP, ST),
        P(AXES, None),
        P(AXES, None),
        P(ST, None),
        P(None, ST),
        P(None, None, ST),
        P(),
    )
    return jax.shard_map(
        shards,
        mesh=fine,
        in_specs=placed,
        out_specs=(P(AXES, None), P(None, None, ST), P(None, ST)),
        check_vma=False,
    )
```

```python
import jax
import jax.numpy as jnp
import numpy as np
from jax import lax
from jax.experimental import pallas as pl
from jax.experimental.pallas import tpu as pltpu
from jax.sharding import Mesh, PartitionSpec as P

AXES = ("zh", "x", "yh", "yl", "zl", "c")
SIZES = (4, 4, 4, 2, 2, 2)
Y = ("yh", "yl")
DP = ("zh", "x")
ST = ("yh", "yl", "zl", "c")
F32, BF16 = jnp.float32, jnp.bfloat16
VMEM = pl.BlockSpec(memory_space=pltpu.VMEM)
PARAMS = pltpu.CompilerParams(vmem_limit_bytes=56 * 2**20)


def contract_last(left, right):
    return lax.dot_general(left, right, (((1,), (1,)), ((), ())), preferred_element_type=F32)


def contract_first(left, right):
    return lax.dot_general(left, right, (((0,), (0,)), ((), ())), preferred_element_type=F32)


def exchange(blocks, axes):
    return lax.all_to_all(blocks, axes, 0, 0, tiled=True)


def spread(block, axes, count):
    return exchange(jnp.broadcast_to(block[None], (count,) + block.shape), axes)


def swap_cores(array):
    return lax.ppermute(array, "c", [(0, 1), (1, 0)])


def halve(array, dim, axis, size, bit):
    mine = lax.axis_index(axis) // bit % 2
    kept = lax.dynamic_index_in_dim(array, mine, dim, False)
    sent = lax.dynamic_index_in_dim(array, 1 - mine, dim, False)
    return kept + lax.ppermute(sent, axis, [(i, i ^ bit) for i in range(size)])


def by_permutes(whole):
    zh = lax.axis_index("zh")
    parts = []
    for step in range(4):
        block = lax.dynamic_slice_in_dim(whole, (zh + step) % 4 * 128, 128, 1)
        parts.append(block if step == 0 else lax.ppermute(block, "zh", [(i, (i + step) % 4) for i in range(4)]))
    return parts


def band_pairs():
    index = np.arange(512).reshape(SIZES)
    pairs = []
    for zh in range(4):
        for x in range(4):
            for yh in range(4):
                for yl in range(2):
                    for zl in range(2):
                        for c in range(2):
                            source = index[yh, x, zh, yl, zl, c]
                            pairs.append((int(source), int(index[zh, x, yh, yl, zl, c])))
    return pairs


def join(array, axis):
    other = lax.ppermute(array, axis, [(0, 1), (1, 0)])
    first = lax.axis_index(axis) == 0
    return jnp.where(first, jnp.concatenate([array, other]), jnp.concatenate([other, array]))


def partial_hidden(rows, weights, a_down):
    rows = rows[:, :2048].reshape(512, 4, 512)
    total = lax.dot_general(weights, rows, (((0, 2), (1, 2)), ((), ())), preferred_element_type=F32)
    rank = total[832:].astype(BF16)
    whole = total[:832] + jnp.dot(a_down, rank, preferred_element_type=F32)
    return whole.astype(BF16)


def adapter_sums(parts, gate_ref, up_ref, saved_ref, b_gate_ref, b_up_ref):
    grad_hidden = (parts[0].astype(F32) + parts[1].astype(F32)) + (parts[2].astype(F32) + parts[3].astype(F32))
    grad_gate = (grad_hidden * gate_ref[...]).astype(BF16)
    grad_up = (grad_hidden * up_ref[...]).astype(BF16)
    rank = jnp.dot(b_gate_ref[...], grad_gate, preferred_element_type=F32)
    rank = rank + jnp.dot(b_up_ref[...], grad_up, preferred_element_type=F32)
    return rank.T, contract_last(saved_ref[:64, :], grad_gate), contract_last(saved_ref[64:, :], grad_up)


def own_kernel(parts_ref, gate_ref, up_ref, saved_ref, b_gate_ref, b_up_ref, rank_ref, sums_ref):
    rank, into_gate, into_up = adapter_sums(parts_ref[...], gate_ref, up_ref, saved_ref, b_gate_ref, b_up_ref)
    rank_ref[...] = rank
    sums_ref[:64, :] = into_gate
    sums_ref[64:, :] = into_up


def other_kernel(
    a_ref, b_ref, c_ref, d_ref, gate_ref, up_ref, saved_ref, b_gate_ref, b_up_ref, own_sums_ref, down_ref, rank_ref, sums_ref
):
    parts = (a_ref[...], b_ref[...], c_ref[...], d_ref[...])
    rank, into_gate, into_up = adapter_sums(parts, gate_ref, up_ref, saved_ref, b_gate_ref, b_up_ref)
    rank_ref[...] = rank
    sums_ref[:, :128] = down_ref[...]
    sums_ref[:64, 128:] = (own_sums_ref[:64, :] + into_gate).astype(BF16)
    sums_ref[64:, 128:] = (own_sums_ref[64:, :] + into_up).astype(BF16)


def own_terms(*operands):
    return pl.pallas_call(
        own_kernel,
        out_shape=(jax.ShapeDtypeStruct((128, 128), F32), jax.ShapeDtypeStruct((128, 832), F32)),
        in_specs=[VMEM] * 6,
        out_specs=(VMEM, VMEM),
        compiler_params=PARAMS,
        cost_estimate=pl.CostEstimate(flops=10**8, bytes_accessed=3 * 2**20, transcendentals=0),
    )(*operands)


def other_terms(*operands):
    return pl.pallas_call(
        other_kernel,
        out_shape=(jax.ShapeDtypeStruct((128, 128), F32), jax.ShapeDtypeStruct((128, 960), BF16)),
        in_specs=[VMEM] * 11,
        out_specs=(VMEM, VMEM),
        compiler_params=PARAMS,
        cost_estimate=pl.CostEstimate(flops=10**8, bytes_accessed=3 * 2**20, transcendentals=0),
    )(*operands)


def factor_kernel(core_ref, gate_ref, up_ref, gate_out, up_out):
    core = core_ref[0]
    gate_rows = gate_ref[...].astype(F32).reshape(16, 2, 8, 832)
    up_rows = up_ref[...].astype(F32).reshape(16, 2, 8, 832)
    for which in range(2):
        slot = core if which == 0 else 1 - core
        gate_value = gate_rows[:, which].reshape(128, 832)
        sigmoid_gate = jax.nn.sigmoid(gate_value)
        up_out[slot] = (gate_value * sigmoid_gate).T
        slope = sigmoid_gate * (1.0 + gate_value * (1.0 - sigmoid_gate))
        gate_out[slot] = (up_rows[:, which].reshape(128, 832) * slope).T


def factors(core, gate_pre, up_pre):
    shape = jax.ShapeDtypeStruct((2, 832, 128), F32)
    return pl.pallas_call(
        factor_kernel,
        out_shape=(shape, shape),
        in_specs=[pl.BlockSpec(memory_space=pltpu.SMEM), VMEM, VMEM],
        out_specs=(VMEM, VMEM),
        compiler_params=PARAMS,
        cost_estimate=pl.CostEstimate(flops=10**7, bytes_accessed=3 * 2**20, transcendentals=256 * 832),
    )(core.reshape(1), gate_pre, up_pre)


def saved_kernel(place_ref, own_band_ref, other_band_ref, own_ranks_ref, other_ranks_ref, saved_ref, down_ref):
    down = contract_first(own_ranks_ref[:, 128:192], own_band_ref[...])
    down = down + contract_first(other_ranks_ref[:, 128:192], other_band_ref[...])
    down_ref[...] = jnp.where(place_ref[2] == 1, down, 0.0).astype(BF16)
    window = pl.ds(pl.multiple_of(place_ref[1] * 128, 128), 128)
    saved_ref[0] = own_ranks_ref[window, :128].T
    saved_ref[1] = other_ranks_ref[window, :128].T


def saved_terms(place, own_rows, other_rows):
    band = pl.BlockSpec((512, 256), lambda i, place: (0, place[0]))
    ranks = pl.BlockSpec((512, 256), lambda i, place: (0, 8))
    return pl.pallas_call(
        saved_kernel,
        grid_spec=pltpu.PrefetchScalarGridSpec(
            num_scalar_prefetch=1,
            grid=(1,),
            in_specs=[band, band, ranks, ranks],
            out_specs=(
                pl.BlockSpec((2, 128, 128), lambda i, place: (0, 0, 0)),
                pl.BlockSpec((64, 256), lambda i, place: (0, 0)),
            ),
        ),
        out_shape=(jax.ShapeDtypeStruct((2, 128, 128), BF16), jax.ShapeDtypeStruct((64, 256), BF16)),
        compiler_params=PARAMS,
        cost_estimate=pl.CostEstimate(flops=2 * 1024 * 64 * 256, bytes_accessed=2**20, transcendentals=0),
    )(place, own_rows, other_rows, own_rows, other_rows)


def shards(grad_out, w_down, gate_pre, up_pre, rank_in, rank_hidden, a_down, b_down, b_in, a_in):
    core = lax.axis_index("c")
    zh = lax.axis_index("zh")
    station = lax.axis_index(ST)

    ranks = jnp.concatenate([rank_in, rank_hidden, jnp.zeros((8, 64), BF16)], axis=1)
    quarters = grad_out.reshape(8, 4, 2048).transpose(1, 0, 2)
    quarters = jnp.concatenate([quarters, jnp.broadcast_to(ranks[None], (4, 8, 256))], axis=2)
    blocks = jnp.broadcast_to(quarters[:, None], (4, 2, 8, 2304)).reshape(8, 8, 2304)
    from_z = exchange(blocks, ("zh", "zl"))
    gate_factor, up_factor = factors(core, gate_pre, up_pre)
    none = jnp.zeros((64, 832), BF16)
    b_gate, b_up = jnp.concatenate([b_in[0], none]), jnp.concatenate([none, b_in[1]])
    w_copies = jnp.broadcast_to(w_down[None], (4, 832, 512))
    from_z, w_copies = lax.optimization_barrier((from_z, w_copies))
    own = lax.all_gather(from_z.reshape(4, 16, 2304), Y, axis=1, tiled=True)
    weights = exchange(w_copies.reshape(3328, 512), "x").reshape(4, 832, 512)
    b_down, gate_factor, up_factor = lax.optimization_barrier((b_down, gate_factor, up_factor))
    bands = lax.ppermute(b_down, AXES, band_pairs())[None]
    bands = join(join(join(bands, "c"), "zl"), "yl")
    bands = bands.reshape(4, 2, 64, 256).transpose(0, 2, 1, 3).reshape(4, 64, 512)
    own, bands, a_down, b_gate, b_up = lax.optimization_barrier((own, bands, a_down, b_gate, b_up))
    own_rows = own.reshape(512, 2304)
    other_rows = swap_cores(own_rows)
    weights = jnp.concatenate([weights, bands], axis=1)
    own_partial = partial_hidden(own_rows, weights, a_down)
    own_parts = exchange(own_partial.reshape(832, 4, 128).transpose(1, 0, 2), "zh")
    other_partial = partial_hidden(other_rows, weights, a_down)
    other_parts = by_permutes(other_partial)

    place = jnp.stack([station % 8, zh, (station // 8 == zh).astype(jnp.int32)])
    place, _ = lax.optimization_barrier((place, other_partial))
    saved, partial_down = saved_terms(place, own_rows, other_rows)
    partial_down = partial_down.reshape(128, 128)
    own_rank, own_sums = own_terms(own_parts, gate_factor[0], up_factor[0], saved[0], b_gate, b_up)
    other_rank, sums = other_terms(
        *other_parts, gate_factor[1], up_factor[1], saved[1], b_gate, b_up, own_sums, partial_down
    )
    sums = jnp.sum(exchange(sums.reshape(16, 8, 960), DP).astype(F32), axis=0).astype(BF16)
    rank_grad = (own_rank + swap_cores(other_rank)).reshape(8, 2, 8, 128)
    rank_grad = halve(rank_grad, 1, "zl", 2, 1)
    rank_grad = halve(rank_grad.reshape(4, 2, 8, 128), 1, "yl", 2, 1)
    rank_grad = halve(rank_grad.reshape(2, 2, 8, 128), 1, "yh", 4, 1)
    rank_grad = halve(rank_grad.reshape(2, 8, 128), 0, "yh", 4, 2)
    rank_grad = rank_grad.astype(BF16)
    sums = spread(sums, DP, 16).astype(F32)
    grad_b_in = sums[:, :, 128:].reshape(2, 64, 832)
    grad_b_down = sums[:, :, :128].reshape(64, 256)
    input_grad = contract_last(rank_grad, a_in).astype(BF16)
    return (input_grad, grad_b_in, grad_b_down)


def solution(mesh):
    fine = Mesh(mesh.devices.reshape(SIZES), AXES)
    placed = (
        P(AXES, None),
        P(ST, DP),
        P(DP, ST),
        P(DP, ST),
        P(AXES, None),
        P(AXES, None),
        P(ST, None),
        P(None, ST),
        P(None, None, ST),
        P(),
    )
    return jax.shard_map(
        shards,
        mesh=fine,
        in_specs=placed,
        out_specs=(P(AXES, None), P(None, None, ST), P(None, ST)),
        check_vma=False,
    )
```

```python
import jax
import jax.numpy as jnp
import numpy as np
from jax import lax
from jax.experimental import pallas as pl
from jax.experimental.pallas import tpu as pltpu
from jax.sharding import Mesh, PartitionSpec as P

AXES = ("zh", "x", "yh", "yl", "zl", "c")
SIZES = (4, 4, 4, 2, 2, 2)
Y = ("yh", "yl")
DP = ("zh", "x")
ST = ("yh", "yl", "zl", "c")
F32, BF16 = jnp.float32, jnp.bfloat16
VMEM = pl.BlockSpec(memory_space=pltpu.VMEM)
PARAMS = pltpu.CompilerParams(vmem_limit_bytes=56 * 2**20)


def contract_last(left, right):
    return lax.dot_general(left, right, (((1,), (1,)), ((), ())), preferred_element_type=F32)


def contract_first(left, right):
    return lax.dot_general(left, right, (((0,), (0,)), ((), ())), preferred_element_type=F32)


def exchange(blocks, axes):
    return lax.all_to_all(blocks, axes, 0, 0, tiled=True)


def spread(block, axes, count):
    return exchange(jnp.broadcast_to(block[None], (count,) + block.shape), axes)


def swap_cores(array):
    return lax.ppermute(array, "c", [(0, 1), (1, 0)])


def halve(array, dim, axis, size, bit):
    mine = lax.axis_index(axis) // bit % 2
    kept = lax.dynamic_index_in_dim(array, mine, dim, False)
    sent = lax.dynamic_index_in_dim(array, 1 - mine, dim, False)
    return kept + lax.ppermute(sent, axis, [(i, i ^ bit) for i in range(size)])


def by_permutes(whole):
    zh = lax.axis_index("zh")
    parts = []
    for step in range(4):
        block = lax.dynamic_slice_in_dim(whole, (zh + step) % 4 * 128, 128, 1)
        parts.append(block if step == 0 else lax.ppermute(block, "zh", [(i, (i + step) % 4) for i in range(4)]))
    return parts


def band_pairs():
    index = np.arange(512).reshape(SIZES)
    pairs = []
    for zh in range(4):
        for x in range(4):
            for yh in range(4):
                for yl in range(2):
                    for zl in range(2):
                        for c in range(2):
                            source = index[yh, x, zh, yl, zl, c]
                            pairs.append((int(source), int(index[zh, x, yh, yl, zl, c])))
    return pairs


def join(array, axis):
    other = lax.ppermute(array, axis, [(0, 1), (1, 0)])
    first = lax.axis_index(axis) == 0
    return jnp.where(first, jnp.concatenate([array, other]), jnp.concatenate([other, array]))


def partial_hidden(rows, weights, a_down):
    rows = rows[:, :2048].reshape(512, 4, 512)
    total = lax.dot_general(weights, rows, (((0, 2), (1, 2)), ((), ())), preferred_element_type=F32)
    rank = total[832:].astype(BF16)
    whole = total[:832] + jnp.dot(a_down, rank, preferred_element_type=F32)
    return whole.astype(BF16)


def adapter_sums(parts, gate_ref, up_ref, saved_ref, b_gate_ref, b_up_ref):
    grad_hidden = (parts[0].astype(F32) + parts[1].astype(F32)) + (parts[2].astype(F32) + parts[3].astype(F32))
    grad_gate = (grad_hidden * gate_ref[...]).astype(BF16)
    grad_up = (grad_hidden * up_ref[...]).astype(BF16)
    rank = jnp.dot(b_gate_ref[...], grad_gate, preferred_element_type=F32)
    rank = rank + jnp.dot(b_up_ref[...], grad_up, preferred_element_type=F32)
    return rank.T, contract_last(saved_ref[:64, :], grad_gate), contract_last(saved_ref[64:, :], grad_up)


def first_kernel(parts_ref, gate_ref, up_ref, saved_ref, b_gate_ref, b_up_ref, rank_ref, sums_ref):
    rank, into_gate, into_up = adapter_sums(parts_ref[...], gate_ref, up_ref, saved_ref, b_gate_ref, b_up_ref)
    rank_ref[...] = rank
    sums_ref[:64, :] = into_gate
    sums_ref[64:, :] = into_up


def last_kernel(
    a_ref, b_ref, c_ref, d_ref, gate_ref, up_ref, saved_ref, b_gate_ref, b_up_ref, first_ref, down_ref, rank_ref, sums_ref
):
    parts = (a_ref[...], b_ref[...], c_ref[...], d_ref[...])
    rank, into_gate, into_up = adapter_sums(parts, gate_ref, up_ref, saved_ref, b_gate_ref, b_up_ref)
    rank_ref[...] = rank
    sums_ref[:, :128] = down_ref[...]
    sums_ref[:64, 128:] = (first_ref[:64, :] + into_gate).astype(BF16)
    sums_ref[64:, 128:] = (first_ref[64:, :] + into_up).astype(BF16)


def first_terms(*operands):
    return pl.pallas_call(
        first_kernel,
        out_shape=(jax.ShapeDtypeStruct((128, 128), F32), jax.ShapeDtypeStruct((128, 832), F32)),
        in_specs=[VMEM] * 6,
        out_specs=(VMEM, VMEM),
        compiler_params=PARAMS,
        cost_estimate=pl.CostEstimate(flops=10**8, bytes_accessed=3 * 2**20, transcendentals=0),
    )(*operands)


def last_terms(*operands):
    return pl.pallas_call(
        last_kernel,
        out_shape=(jax.ShapeDtypeStruct((128, 128), F32), jax.ShapeDtypeStruct((128, 960), BF16)),
        in_specs=[VMEM] * 11,
        out_specs=(VMEM, VMEM),
        compiler_params=PARAMS,
        cost_estimate=pl.CostEstimate(flops=10**8, bytes_accessed=3 * 2**20, transcendentals=0),
    )(*operands)


def factor_kernel(core_ref, gate_ref, up_ref, own_gate_ref, own_up_ref, other_gate_ref, other_up_ref):
    gate_rows = gate_ref[...].astype(F32).reshape(16, 2, 8, 832)
    up_rows = up_ref[...].astype(F32).reshape(16, 2, 8, 832)
    first = core_ref[0] == 0

    def tokens(rows, own):
        zero, one = rows[:, 0].reshape(128, 832), rows[:, 1].reshape(128, 832)
        return jnp.where(first, zero, one) if own else jnp.where(first, one, zero)

    for own, gate_out, up_out in ((True, own_gate_ref, own_up_ref), (False, other_gate_ref, other_up_ref)):
        gate_value = tokens(gate_rows, own)
        sigmoid_gate = jax.nn.sigmoid(gate_value)
        up_out[...] = (gate_value * sigmoid_gate).T
        slope = sigmoid_gate * (1.0 + gate_value * (1.0 - sigmoid_gate))
        gate_out[...] = (tokens(up_rows, own) * slope).T


def factors(core, gate_pre, up_pre):
    shape = jax.ShapeDtypeStruct((832, 128), F32)
    return pl.pallas_call(
        factor_kernel,
        out_shape=(shape,) * 4,
        in_specs=[pl.BlockSpec(memory_space=pltpu.SMEM), VMEM, VMEM],
        out_specs=(VMEM,) * 4,
        compiler_params=PARAMS,
        cost_estimate=pl.CostEstimate(flops=10**7, bytes_accessed=3 * 2**20, transcendentals=256 * 832),
    )(core.reshape(1), gate_pre, up_pre)


def saved_kernel(place_ref, own_band_ref, other_band_ref, own_ranks_ref, other_ranks_ref, own_saved_ref, other_saved_ref, down_ref):
    down = contract_first(own_ranks_ref[:, 128:192], own_band_ref[...])
    down = down + contract_first(other_ranks_ref[:, 128:192], other_band_ref[...])
    down_ref[...] = jnp.where(place_ref[2] == 1, down, 0.0).astype(BF16)
    window = pl.ds(pl.multiple_of(place_ref[1] * 128, 128), 128)
    own_saved_ref[...] = own_ranks_ref[window, :128].T
    other_saved_ref[...] = other_ranks_ref[window, :128].T


def saved_terms(place, own_rows, other_rows):
    band = pl.BlockSpec((512, 256), lambda i, place: (0, place[0]))
    ranks = pl.BlockSpec((512, 256), lambda i, place: (0, 8))
    return pl.pallas_call(
        saved_kernel,
        grid_spec=pltpu.PrefetchScalarGridSpec(
            num_scalar_prefetch=1,
            grid=(1,),
            in_specs=[band, band, ranks, ranks],
            out_specs=(
                pl.BlockSpec((128, 128), lambda i, place: (0, 0)),
                pl.BlockSpec((128, 128), lambda i, place: (0, 0)),
                pl.BlockSpec((64, 256), lambda i, place: (0, 0)),
            ),
        ),
        out_shape=(
            jax.ShapeDtypeStruct((128, 128), BF16),
            jax.ShapeDtypeStruct((128, 128), BF16),
            jax.ShapeDtypeStruct((64, 256), BF16),
        ),
        compiler_params=PARAMS,
        cost_estimate=pl.CostEstimate(flops=2 * 1024 * 64 * 256, bytes_accessed=2**20, transcendentals=0),
    )(place, own_rows, other_rows, own_rows, other_rows)


def shards(grad_out, w_down, gate_pre, up_pre, rank_in, rank_hidden, a_down, b_down, b_in, a_in):
    core = lax.axis_index("c")
    zh = lax.axis_index("zh")
    station = lax.axis_index(ST)

    ranks = jnp.concatenate([rank_in, rank_hidden, jnp.zeros((8, 64), BF16)], axis=1)
    quarters = grad_out.reshape(8, 4, 2048).transpose(1, 0, 2)
    quarters = jnp.concatenate([quarters, jnp.broadcast_to(ranks[None], (4, 8, 256))], axis=2)
    blocks = jnp.broadcast_to(quarters[:, None], (4, 2, 8, 2304)).reshape(8, 8, 2304)
    from_z = exchange(blocks, ("zh", "zl"))
    own_gate, own_up, other_gate, other_up = factors(core, gate_pre, up_pre)
    none = jnp.zeros((64, 832), BF16)
    b_gate, b_up = jnp.concatenate([b_in[0], none]), jnp.concatenate([none, b_in[1]])
    w_copies = jnp.broadcast_to(w_down[None], (4, 832, 512))
    _, w_copies = lax.optimization_barrier((from_z, w_copies))
    own = lax.all_gather(from_z.reshape(4, 16, 2304), Y, axis=1, tiled=True)
    weights = exchange(w_copies.reshape(3328, 512), "x").reshape(4, 832, 512)
    b_down, own_gate, own_up, other_gate, other_up = lax.optimization_barrier((b_down, own_gate, own_up, other_gate, other_up))
    bands = lax.ppermute(b_down, AXES, band_pairs())[None]
    bands = join(join(join(bands, "c"), "zl"), "yl")
    bands = bands.reshape(4, 2, 64, 256).transpose(0, 2, 1, 3).reshape(4, 64, 512)
    own, bands, a_down, b_gate, b_up = lax.optimization_barrier((own, bands, a_down, b_gate, b_up))
    own_rows = own.reshape(512, 2304)
    other_rows = swap_cores(own_rows)
    weights = jnp.concatenate([weights, bands], axis=1)
    own_partial = partial_hidden(own_rows, weights, a_down)
    own_parts = exchange(own_partial.reshape(832, 4, 128).transpose(1, 0, 2), "zh")
    other_partial = partial_hidden(other_rows, weights, a_down)
    other_parts = by_permutes(other_partial)

    place = jnp.stack([station % 8, zh, (station // 8 == zh).astype(jnp.int32)])
    place, _ = lax.optimization_barrier((place, other_partial))
    own_saved, other_saved, partial_down = saved_terms(place, own_rows, other_rows)
    partial_down = partial_down.reshape(128, 128)
    own_rank, first = first_terms(own_parts, own_gate, own_up, own_saved, b_gate, b_up)
    other_rank, sums = last_terms(
        *other_parts, other_gate, other_up, other_saved, b_gate, b_up, first, partial_down
    )
    sums = jnp.sum(exchange(sums.reshape(16, 8, 960), DP).astype(F32), axis=0).astype(BF16)
    rank_grad = (own_rank + swap_cores(other_rank)).reshape(8, 2, 8, 128)
    rank_grad = halve(rank_grad, 1, "zl", 2, 1)
    rank_grad = halve(rank_grad.reshape(4, 2, 8, 128), 1, "yl", 2, 1)
    rank_grad = halve(rank_grad.reshape(2, 2, 8, 128), 1, "yh", 4, 1)
    rank_grad = halve(rank_grad.reshape(2, 8, 128), 0, "yh", 4, 2)
    rank_grad = rank_grad.astype(BF16)
    sums = spread(sums, DP, 16).astype(F32)
    grad_b_in = sums[:, :, 128:].reshape(2, 64, 832)
    grad_b_down = sums[:, :, :128].reshape(64, 256)
    input_grad = contract_last(rank_grad, a_in).astype(BF16)
    return (input_grad, grad_b_in, grad_b_down)


def solution(mesh):
    fine = Mesh(mesh.devices.reshape(SIZES), AXES)
    placed = (
        P(AXES, None),
        P(ST, DP),
        P(DP, ST),
        P(DP, ST),
        P(AXES, None),
        P(AXES, None),
        P(ST, None),
        P(None, ST),
        P(None, None, ST),
        P(),
    )
    return jax.shard_map(
        shards,
        mesh=fine,
        in_specs=placed,
        out_specs=(P(AXES, None), P(None, None, ST), P(None, ST)),
        check_vma=False,
    )
```

```python
import jax
import jax.numpy as jnp
import numpy as np
from jax import lax
from jax.experimental import pallas as pl
from jax.experimental.pallas import tpu as pltpu
from jax.sharding import Mesh, PartitionSpec as P

AXES = ("zh", "x", "yh", "yl", "zl", "c")
SIZES = (4, 4, 4, 2, 2, 2)
Y = ("yh", "yl")
DP = ("zh", "x")
ST = ("yh", "yl", "zl", "c")
F32, BF16 = jnp.float32, jnp.bfloat16
VMEM = pl.BlockSpec(memory_space=pltpu.VMEM)
PARAMS = pltpu.CompilerParams(vmem_limit_bytes=56 * 2**20)


def contract_last(left, right):
    return lax.dot_general(left, right, (((1,), (1,)), ((), ())), preferred_element_type=F32)


def contract_first(left, right):
    return lax.dot_general(left, right, (((0,), (0,)), ((), ())), preferred_element_type=F32)


def exchange(blocks, axes):
    return lax.all_to_all(blocks, axes, 0, 0, tiled=True)


def spread(block, axes, count):
    return exchange(jnp.broadcast_to(block[None], (count,) + block.shape), axes)


def swap_cores(array):
    return lax.ppermute(array, "c", [(0, 1), (1, 0)])


def halve(array, dim, axis, size, bit):
    mine = lax.axis_index(axis) // bit % 2
    kept = lax.dynamic_index_in_dim(array, mine, dim, False)
    sent = lax.dynamic_index_in_dim(array, 1 - mine, dim, False)
    return kept + lax.ppermute(sent, axis, [(i, i ^ bit) for i in range(size)])


def by_permutes(whole):
    zh = lax.axis_index("zh")
    parts = []
    for step in range(4):
        block = lax.dynamic_slice_in_dim(whole, (zh + step) % 4 * 128, 128, 1)
        parts.append(block if step == 0 else lax.ppermute(block, "zh", [(i, (i + step) % 4) for i in range(4)]))
    return parts


def band_pairs():
    index = np.arange(512).reshape(SIZES)
    pairs = []
    for zh in range(4):
        for x in range(4):
            for yh in range(4):
                for yl in range(2):
                    for zl in range(2):
                        for c in range(2):
                            source = index[yh, x, zh, yl, zl, c]
                            pairs.append((int(source), int(index[zh, x, yh, yl, zl, c])))
    return pairs


def join(array, axis):
    other = lax.ppermute(array, axis, [(0, 1), (1, 0)])
    first = lax.axis_index(axis) == 0
    return jnp.where(first, jnp.concatenate([array, other]), jnp.concatenate([other, array]))


def partial_hidden(rows, weights, a_down):
    rows = rows[:, :2048].reshape(512, 4, 512)
    total = lax.dot_general(weights, rows, (((0, 2), (1, 2)), ((), ())), preferred_element_type=F32)
    rank = total[832:].astype(BF16)
    whole = total[:832] + jnp.dot(a_down, rank, preferred_element_type=F32)
    return whole.astype(BF16)


def adapter_sums(parts, gate_ref, up_ref, saved_ref, b_gate_ref, b_up_ref):
    grad_hidden = (parts[0].astype(F32) + parts[1].astype(F32)) + (parts[2].astype(F32) + parts[3].astype(F32))
    grad_gate = (grad_hidden * gate_ref[...]).astype(BF16)
    grad_up = (grad_hidden * up_ref[...]).astype(BF16)
    rank = jnp.dot(b_gate_ref[...], grad_gate, preferred_element_type=F32)
    rank = rank + jnp.dot(b_up_ref[...], grad_up, preferred_element_type=F32)
    return rank.T, contract_last(saved_ref[:64, :], grad_gate), contract_last(saved_ref[64:, :], grad_up)


def first_kernel(parts_ref, gate_ref, up_ref, saved_ref, b_gate_ref, b_up_ref, rank_ref, sums_ref):
    rank, into_gate, into_up = adapter_sums(parts_ref[...], gate_ref, up_ref, saved_ref, b_gate_ref, b_up_ref)
    rank_ref[...] = rank
    sums_ref[:64, :] = into_gate
    sums_ref[64:, :] = into_up


def last_kernel(
    a_ref, b_ref, c_ref, d_ref, gate_ref, up_ref, saved_ref, b_gate_ref, b_up_ref, first_ref, down_ref, rank_ref, sums_ref
):
    parts = (a_ref[...], b_ref[...], c_ref[...], d_ref[...])
    rank, into_gate, into_up = adapter_sums(parts, gate_ref, up_ref, saved_ref, b_gate_ref, b_up_ref)
    rank_ref[...] = rank
    sums_ref[:, :128] = down_ref[...]
    sums_ref[:64, 128:] = (first_ref[:64, :] + into_gate).astype(BF16)
    sums_ref[64:, 128:] = (first_ref[64:, :] + into_up).astype(BF16)


def first_terms(*operands):
    return pl.pallas_call(
        first_kernel,
        out_shape=(jax.ShapeDtypeStruct((128, 128), F32), jax.ShapeDtypeStruct((128, 832), F32)),
        in_specs=[VMEM] * 6,
        out_specs=(VMEM, VMEM),
        compiler_params=PARAMS,
        cost_estimate=pl.CostEstimate(flops=10**8, bytes_accessed=3 * 2**20, transcendentals=0),
    )(*operands)


def last_terms(*operands):
    return pl.pallas_call(
        last_kernel,
        out_shape=(jax.ShapeDtypeStruct((128, 128), F32), jax.ShapeDtypeStruct((128, 960), BF16)),
        in_specs=[VMEM] * 11,
        out_specs=(VMEM, VMEM),
        compiler_params=PARAMS,
        cost_estimate=pl.CostEstimate(flops=10**8, bytes_accessed=3 * 2**20, transcendentals=0),
    )(*operands)


def factor_kernel(core_ref, gate_ref, up_ref, own_gate_ref, own_up_ref, other_gate_ref, other_up_ref):
    gate_rows = gate_ref[...].astype(F32).reshape(16, 2, 8, 832)
    up_rows = up_ref[...].astype(F32).reshape(16, 2, 8, 832)
    first = core_ref[0] == 0

    def tokens(rows, own):
        zero, one = rows[:, 0].reshape(128, 832), rows[:, 1].reshape(128, 832)
        return jnp.where(first, zero, one) if own else jnp.where(first, one, zero)

    for own, gate_out, up_out in ((True, own_gate_ref, own_up_ref), (False, other_gate_ref, other_up_ref)):
        gate_value = tokens(gate_rows, own)
        sigmoid_gate = jax.nn.sigmoid(gate_value)
        up_out[...] = (gate_value * sigmoid_gate).T
        slope = sigmoid_gate * (1.0 + gate_value * (1.0 - sigmoid_gate))
        gate_out[...] = (tokens(up_rows, own) * slope).T


def factors(core, gate_pre, up_pre):
    shape = jax.ShapeDtypeStruct((832, 128), F32)
    return pl.pallas_call(
        factor_kernel,
        out_shape=(shape,) * 4,
        in_specs=[pl.BlockSpec(memory_space=pltpu.SMEM), VMEM, VMEM],
        out_specs=(VMEM,) * 4,
        compiler_params=PARAMS,
        cost_estimate=pl.CostEstimate(flops=10**7, bytes_accessed=3 * 2**20, transcendentals=256 * 832),
    )(core.reshape(1), gate_pre, up_pre)


def saved_kernel(place_ref, own_band_ref, other_band_ref, own_ranks_ref, other_ranks_ref, own_saved_ref, other_saved_ref, down_ref):
    down = contract_first(own_ranks_ref[:, 128:192], own_band_ref[...])
    down = down + contract_first(other_ranks_ref[:, 128:192], other_band_ref[...])
    down_ref[...] = jnp.where(place_ref[2] == 1, down, 0.0).astype(BF16)
    window = pl.ds(pl.multiple_of(place_ref[1] * 128, 128), 128)
    own_saved_ref[...] = own_ranks_ref[window, :128].T
    other_saved_ref[...] = other_ranks_ref[window, :128].T


def saved_terms(place, own_rows, other_rows):
    band = pl.BlockSpec((512, 256), lambda i, place: (0, place[0]))
    ranks = pl.BlockSpec((512, 256), lambda i, place: (0, 8))
    return pl.pallas_call(
        saved_kernel,
        grid_spec=pltpu.PrefetchScalarGridSpec(
            num_scalar_prefetch=1,
            grid=(1,),
            in_specs=[band, band, ranks, ranks],
            out_specs=(
                pl.BlockSpec((128, 128), lambda i, place: (0, 0)),
                pl.BlockSpec((128, 128), lambda i, place: (0, 0)),
                pl.BlockSpec((64, 256), lambda i, place: (0, 0)),
            ),
        ),
        out_shape=(
            jax.ShapeDtypeStruct((128, 128), BF16),
            jax.ShapeDtypeStruct((128, 128), BF16),
            jax.ShapeDtypeStruct((64, 256), BF16),
        ),
        compiler_params=PARAMS,
        cost_estimate=pl.CostEstimate(flops=2 * 1024 * 64 * 256, bytes_accessed=2**20, transcendentals=0),
    )(place, own_rows, other_rows, own_rows, other_rows)


def shards(grad_out, w_down, gate_pre, up_pre, rank_in, rank_hidden, a_down, b_down, b_in, a_in):
    core = lax.axis_index("c")
    zh = lax.axis_index("zh")
    station = lax.axis_index(ST)

    ranks = jnp.concatenate([rank_in, rank_hidden, jnp.zeros((8, 64), BF16)], axis=1)
    quarters = grad_out.reshape(8, 4, 2048).transpose(1, 0, 2)
    quarters = jnp.concatenate([quarters, jnp.broadcast_to(ranks[None], (4, 8, 256))], axis=2)
    blocks = jnp.broadcast_to(quarters[:, None], (4, 2, 8, 2304)).reshape(8, 8, 2304)
    from_z = exchange(blocks, ("zh", "zl"))
    own_gate, own_up, other_gate, other_up = factors(core, gate_pre, up_pre)
    none = jnp.zeros((64, 832), BF16)
    b_gate, b_up = jnp.concatenate([b_in[0], none]), jnp.concatenate([none, b_in[1]])
    w_copies = jnp.broadcast_to(w_down[None], (4, 832, 512))
    _, w_copies = lax.optimization_barrier((from_z, w_copies))
    own = lax.all_gather(from_z.reshape(4, 16, 2304), Y, axis=1, tiled=True)
    weights = exchange(w_copies.reshape(3328, 512), "x").reshape(4, 832, 512)
    b_down, own_gate, own_up, other_gate, other_up = lax.optimization_barrier((b_down, own_gate, own_up, other_gate, other_up))
    bands = lax.ppermute(b_down, AXES, band_pairs())[None]
    bands = join(join(join(bands, "c"), "zl"), "yl")
    bands = bands.reshape(4, 2, 64, 256).transpose(0, 2, 1, 3).reshape(4, 64, 512)
    own, bands, a_down, b_gate, b_up = lax.optimization_barrier((own, bands, a_down, b_gate, b_up))
    own_rows = own.reshape(512, 2304)
    other_rows = swap_cores(own_rows)
    weights = jnp.concatenate([weights, bands], axis=1)
    own_partial = partial_hidden(own_rows, weights, a_down)
    own_parts = exchange(own_partial.reshape(832, 4, 128).transpose(1, 0, 2), "zh")
    other_partial = partial_hidden(other_rows, weights, a_down)
    other_parts = by_permutes(other_partial)

    place = jnp.stack([station % 8, zh, (station // 8 == zh).astype(jnp.int32)])
    place, _ = lax.optimization_barrier((place, other_partial))
    own_saved, other_saved, partial_down = saved_terms(place, own_rows, other_rows)
    partial_down = partial_down.reshape(128, 128)
    own_rank, first = first_terms(own_parts, own_gate, own_up, own_saved, b_gate, b_up)
    other_rank, sums = last_terms(
        *other_parts, other_gate, other_up, other_saved, b_gate, b_up, first, partial_down
    )
    sums = jnp.sum(exchange(sums.reshape(16, 8, 960), DP).astype(F32), axis=0).astype(BF16)
    rank_grad = (own_rank + swap_cores(other_rank)).reshape(2, 2, 2, 2, 8, 128)
    rank_grad = halve(rank_grad, 0, "yh", 4, 2)
    rank_grad = halve(rank_grad, 2, "zl", 2, 1)
    rank_grad = halve(rank_grad, 0, "yh", 4, 1)
    rank_grad = halve(rank_grad, 0, "yl", 2, 1)
    rank_grad = rank_grad.astype(BF16)
    sums = spread(sums, DP, 16).astype(F32)
    grad_b_in = sums[:, :, 128:].reshape(2, 64, 832)
    grad_b_down = sums[:, :, :128].reshape(64, 256)
    input_grad = contract_last(rank_grad, a_in).astype(BF16)
    return (input_grad, grad_b_in, grad_b_down)


def solution(mesh):
    fine = Mesh(mesh.devices.reshape(SIZES), AXES)
    placed = (
        P(AXES, None),
        P(ST, DP),
        P(DP, ST),
        P(DP, ST),
        P(AXES, None),
        P(AXES, None),
        P(ST, None),
        P(None, ST),
        P(None, None, ST),
        P(),
    )
    return jax.shard_map(
        shards,
        mesh=fine,
        in_specs=placed,
        out_specs=(P(AXES, None), P(None, None, ST), P(None, ST)),
        check_vma=False,
    )
```
